128 devices in a mesh: row: 8 (over z, core), col: 16 (over y, x).
Axes of the slice: x: 4, y: 4, z: 4, core: 2. Of those that a mesh axis runs over, the one named last changes fastest.
Arguments:
- amplitudes: float32 [2048, 8192], P('col', 'row'), may hold values from -6 to 6
- integral_tiles: float32 [128, 128, 1, 128, 128], P(None, ('row', 'col')), may hold values from -0.09375 to 0.09375
- integral_blocks: int32 [128, 128, 1, 2], P(None, ('row', 'col')), may hold values from -1 to 511, as said below
Outputs:
- pair_ladder: float32 [2048, 65536], P('row', 'col')
The draws below stay inside these ranges and needn't reach their ends.
Inputs may be any that keep to these rules, and one draw needn't show every extreme that they name: `integral_blocks`: take a device g of the mesh over row+col (row slowest) with row index r and column index c. Entries [g, d, s, :] describe position j = d + s of the 128 listed tiles of g, held by device d. The positions form 4 groups of 32 in a row; in a live group, position j holds cd tile r * 8 + u, with u the same within the group and different between groups, and ab tile c * 32 + (j mod 32); in an empty group both entries are -1. Live groups come first; a quarter of 4 or more are live on every g, and all 4 on some g. Cd tiles lie below 8 * 8 and ab tiles below 32 * 16.
All inputs are finite; a program needn't handle non-finite values.
Results may differ from the reference program's by a relative error of at most 0.0003.
Values sent between devices are 32-bit elements; how exact they have to be, the bound alone decides.
No kernel may reach another device: no remote copies, remote signals or barrier semaphores. Data moves between devices by JAX's collectives and lax.ppermute only.
A program may use at most 128 MiB of HBM per device.

```python
import jax
import jax.numpy as jnp
from jax import lax

TB = 128
ABT = 32
CD_ROW = 8
GROUPS = 4
PAIRS = 2048
CD = 8192
SLOTS = 128
SHARE = 1
N_ROW = 8
N_COL = 16
DEVICES = 128


def pick_order(device_key):
    return jax.random.permutation(device_key, CD_ROW)[:GROUPS]


def draw_integral_blocks(key, part):
    key = jax.random.fold_in(key, 7)
    key_lives, key_top, key_order = jax.random.split(key, 3)
    live_groups = jax.random.randint(key_lives, (DEVICES,), GROUPS // 4, GROUPS + 1)
    busiest = jax.random.randint(key_top, (), 0, DEVICES)
    device_ids = jnp.arange(DEVICES)
    live_groups = jnp.where(device_ids == busiest, GROUPS, live_groups)
    orderings = jax.vmap(pick_order)(jax.random.split(key_order, DEVICES))
    grid_row = device_ids // N_COL
    grid_col = device_ids % N_COL
    present = jnp.arange(GROUPS)[None, :] < live_groups[:, None]
    cd_groups = jnp.where(present, grid_row[:, None] * CD_ROW + orderings, -1)
    cd_slots = jnp.repeat(cd_groups, ABT, axis=1)
    ab_slots = grid_col[:, None] * ABT + jnp.tile(jnp.arange(ABT), GROUPS)[None, :]
    ab_slots = jnp.where(jnp.repeat(present, ABT, axis=1), ab_slots, -1)
    stacked = jnp.stack([cd_slots, ab_slots], axis=-1).astype(jnp.int32)
    return stacked.reshape(DEVICES, DEVICES, SHARE, 2)


def steps_of(stream_key, dims, pieces, low, top_value):
    level, own = 1.0, jax.random.fold_in(stream_key, 6)
    for position, parts in pieces:
        heights = jnp.exp(jax.random.uniform(jax.random.fold_in(own, position), (parts,), jnp.float32, low / len(pieces), top_value / len(pieces)))
        level = level * jnp.repeat(heights, dims[position] // parts).reshape([-1 if axis == position else 1 for axis in range(len(dims))])
    return level


def normal_values(stream_key, shape, width, most, pieces=(), kind=jnp.bfloat16):
    entries = width * jax.random.normal(stream_key, shape, jnp.float32)
    if pieces:
        entries = entries * steps_of(stream_key, shape, pieces, -0.22, 0.18)
    return jnp.clip(entries, -most, most).astype(kind)


def setup_inputs(seed: int = 0) -> dict:
    key_of = jax.random.split(jax.random.key(seed), 4)
    return {
        "amplitudes": normal_values(key_of[0], (PAIRS, CD), 1.0, 6.0, ((0, 16), (1, 8)), jnp.float32),
        "integral_tiles": normal_values(key_of[1], (DEVICES, DEVICES, SHARE, TB, TB), (N_ROW * GROUPS * TB) ** -0.5, 0.09375, ((1, 128),), jnp.float32),
        "integral_blocks": draw_integral_blocks(jax.random.fold_in(key_of[3], 71), 0),
    }


def reference(amplitudes, integral_tiles, integral_blocks):
    pair_count = amplitudes.shape[0]
    amp_panel = amplitudes.reshape(pair_count, -1, TB)
    grid_tiles = integral_tiles.reshape(-1, SLOTS, TB, TB)
    grid_coords = integral_blocks.reshape(-1, SLOTS, 2)
    running = jnp.zeros((pair_count, ABT * N_COL, TB), jnp.float32)

    def add_block(running, item):
        block_tiles, block_coords = item
        cd_tile = block_coords[:, 0]
        ab_tile = block_coords[:, 1]
        present = cd_tile >= 0
        chosen = jnp.take(amp_panel, jnp.where(present, cd_tile, 0).astype(jnp.int32), axis=1)
        chosen = chosen * present.astype(jnp.float32)[None, :, None]
        products = jnp.einsum("pjx,jxy->pjy", chosen, block_tiles, precision=lax.Precision.HIGHEST)
        running = running.at[:, jnp.where(present, ab_tile, 0).astype(jnp.int32)].add(products)
        return running, None

    running, unused = lax.scan(add_block, running, (grid_tiles, grid_coords))
    return running.reshape(pair_count, -1)
```

```python
import jax
import jax.numpy as jnp
from jax import lax
from jax.experimental import pallas as pl
from jax.experimental.pallas import tpu as pltpu
from jax.sharding import PartitionSpec as P

TB = 128
ABT = 32
CD_ROW = 8
SIDE = 4
N_ROW = 8
N_COL = 16
HALF = 256
PLANE = 512
GCOLS = SIDE * TB
ANYWHERE = ("row", "col")


def col_of(core, a1, a2):
    return jnp.where(core == 0, a2 * SIDE + a1, a1 * SIDE + a2)


def z_shift(step):
    return [(r, ((r // 2 + step) % SIDE) * 2 + r % 2) for r in range(N_ROW)]


def plane_shift(first, step):
    pairs = []
    for r in range(N_ROW):
        for c in range(N_COL):
            y, x = c // SIDE, c % SIDE
            if (r % 2 == 0) == first:
                x = (x + step) % SIDE
            else:
                y = (y + step) % SIDE
            pairs.append((r * N_COL + c, r * N_COL + y * SIDE + x))
    return pairs


def after(values, *deps):
    return lax.optimization_barrier((values, deps))[0]


OTHER_CORE = [(r, r ^ 1) for r in range(N_ROW)]


def params(mib):
    return pltpu.CompilerParams(
        dimension_semantics=("arbitrary",), vmem_limit_bytes=mib * 1024 * 1024
    )


SMALL = pl.CostEstimate(flops=0, bytes_accessed=1024, transcendentals=0)
BIG_MIB, SMALL_MIB = 56, 24


def call(body, grid, table, args, in_specs, out_shape, out_specs, name, mib=BIG_MIB, **more):
    scratch = more.pop("scratch_shapes", [])
    return pl.pallas_call(
        body,
        out_shape=out_shape,
        grid_spec=pltpu.PrefetchScalarGridSpec(
            num_scalar_prefetch=1,
            grid=(grid,),
            in_specs=in_specs,
            out_specs=out_specs,
            scratch_shapes=scratch,
        ),
        compiler_params=params(mib),
        cost_estimate=SMALL,
        name=name,
        **more,
    )(table, *args)


def f32(*shape):
    return jax.ShapeDtypeStruct(shape, jnp.float32)


def fixed(*shape):
    return pl.BlockSpec(shape, lambda j, table: (0,) * len(shape))


def pick_tiles(tiles, table, cols, rows, count):
    def body(table_ref, tiles_ref, *outs):
        for i in range(count):

            @pl.when(pl.program_id(0) == i)
            def _(out=outs[i]):
                for n in range(N_ROW):
                    out[0, n] = tiles_ref[table_ref[rows + n], 0]

    return call(
        body,
        count,
        table,
        [tiles],
        [pl.BlockSpec((N_ROW, 1, TB, TB), lambda j, table_ref: (0, table_ref[cols + j], 0, 0))],
        [f32(1, N_ROW, TB, TB)] * count,
        [fixed(1, N_ROW, TB, TB)] * count,
        "pick_tiles",
    )


def join_tiles(tiles, table, col, rows, passed):
    def body(table_ref, tiles_ref, *refs):
        ins, out = refs[:-1], refs[-1]

        @pl.when(pl.program_id(0) == 0)
        def _():
            for n in range(N_ROW):
                out[0, n] = tiles_ref[table_ref[rows + n], 0]

        for s in range(1, SIDE):

            @pl.when(pl.program_id(0) == s)
            def _(s=s):
                out[...] = ins[s - 1][...]

    block = (1, N_ROW, TB, TB)
    return call(
        body,
        SIDE,
        table,
        [tiles, *passed],
        [pl.BlockSpec((N_ROW, 1, TB, TB), lambda j, table_ref: (0, table_ref[col], 0, 0))]
        + [fixed(*block)] * len(passed),
        f32(SIDE, N_ROW, TB, TB),
        pl.BlockSpec(block, lambda j, table_ref: (j, 0, 0, 0)),
        "join_tiles",
    )


def choose(panels, table, places, live):
    n_ij = panels[0].shape[0]

    def body(table_ref, *refs):
        c = pl.program_id(0)
        out = refs[SIDE]
        for k in range(SIDE):
            at = pl.multiple_of(table_ref[places + c * SIDE + k] * TB, TB)
            tile = refs[k][:, pl.ds(at, TB)]
            listed = table_ref[live + c * SIDE + k] > 0
            out[0, :, k * TB : (k + 1) * TB] = jnp.where(listed, tile, 0.0)

    return call(
        body,
        N_COL,
        table,
        panels,
        [fixed(*p.shape) for p in panels],
        f32(N_COL, n_ij, SIDE * TB),
        pl.BlockSpec((1, n_ij, SIDE * TB), lambda c, table_ref: (c, 0, 0)),
        "choose",
        SMALL_MIB,
    )


def split(x):
    high = x.astype(jnp.bfloat16)
    return high, (x - high.astype(jnp.float32)).astype(jnp.bfloat16)


def product(a_refs, high_ref, low_ref):
    high, low = split(jnp.concatenate([ref[...] for ref in a_refs], axis=1))
    total = jnp.dot(high, low_ref[...], preferred_element_type=jnp.float32)
    total += jnp.dot(low, high_ref[...], preferred_element_type=jnp.float32)
    return total + jnp.dot(high, high_ref[...], preferred_element_type=jnp.float32)


def amp_specs(amps, steps):
    return [
        pl.BlockSpec((HALF, a.shape[1]), lambda i, table_ref: (table_ref[steps + i], 0))
        for a in amps
    ]


DEPTH = N_ROW * TB
TERM = jax.ShapeDtypeStruct((DEPTH, GCOLS), jnp.bfloat16)


def products_away(table, steps, amps, weights):
    def body(table_ref, *refs):
        a_refs, w_refs = refs[: len(amps)], refs[len(amps) : -4]
        half_up, half_down, high_ref, low_ref = refs[-4:]
        i = pl.program_id(0)

        @pl.when(i == 0)
        def _():
            s = 0
            for ref in w_refs:
                for m in range(ref.shape[0]):
                    high, low = split(ref[m].reshape(DEPTH, TB))
                    high_ref[:, s * TB : (s + 1) * TB] = high
                    low_ref[:, s * TB : (s + 1) * TB] = low
                    s += 1

        total = product(a_refs, high_ref, low_ref)

        @pl.when(i == 0)
        def _():
            half_up[...] = total

        @pl.when(i == 1)
        def _():
            half_down[...] = total

    return call(
        body,
        2,
        table,
        [*amps, *weights],
        amp_specs(amps, steps) + [fixed(*w.shape) for w in weights],
        [f32(HALF, GCOLS)] * 2 + [TERM] * 2,
        [fixed(HALF, GCOLS)] * 2 + [fixed(DEPTH, GCOLS)] * 2,
        "products_away",
    )


def products_next(table, steps, amps, terms, from_down, from_up):
    def body(table_ref, *refs):
        a_refs = refs[: len(amps)]
        high_ref, low_ref, f_ref, g_ref, up, down = refs[len(amps) :]
        i = pl.program_id(0)
        total = product(a_refs, high_ref, low_ref)

        @pl.when(i == 0)
        def _():
            up[...] = total + f_ref[...]

        @pl.when(i == 1)
        def _():
            up[...] = total

        @pl.when(i == 2)
        def _():
            down[...] = total

        @pl.when(i == 3)
        def _():
            down[...] = total + g_ref[...]

    return call(
        body,
        4,
        table,
        [*amps, *terms, from_down, from_up],
        amp_specs(amps, steps) + [fixed(DEPTH, GCOLS)] * 2 + [fixed(HALF, GCOLS)] * 2,
        [f32(PLANE, GCOLS)] * 2,
        [
            pl.BlockSpec((HALF, GCOLS), lambda i, table_ref: (jnp.minimum(i, 1), 0)),
            pl.BlockSpec((HALF, GCOLS), lambda i, table_ref: (jnp.maximum(i - 2, 0), 0)),
        ],
        "products_next",
    )


def write_columns(source, out, table_ref, cols, sems):
    copies = []
    for s in range(SIDE):
        at = pl.multiple_of(table_ref[cols + s] * TB, TB)
        copies.append(
            pltpu.make_async_copy(
                source.at[:, pl.ds(s * TB, TB)], out.at[:, pl.ds(at, TB)], sems.at[s]
            )
        )
        copies[-1].start()
    return copies


def products_here(table, steps, amps, terms, from_down, from_up, cols, result, before):
    more = [] if before is None else [before[0]]

    def body(table_ref, *refs):
        a_refs = refs[: len(amps)]
        high_ref, low_ref, f_ref, g_ref = refs[len(amps) : len(amps) + 4]
        theirs, out, mine, sems = refs[-4:]
        i = pl.program_id(0)
        if before is not None:

            @pl.when(i == 0)
            def _():
                copies = write_columns(refs[len(amps) + 4], out, table_ref, before[1], sems)
                for copy in copies:
                    copy.wait()

        total = product(a_refs, high_ref, low_ref) + (f_ref[...] + g_ref[...])

        @pl.when(i == 0)
        def _():
            theirs[...] = total

        @pl.when(i == 1)
        def _():
            mine[...] = total
            for copy in write_columns(mine, out, table_ref, cols, sems):
                copy.wait()

    block = pl.BlockSpec((HALF, GCOLS), lambda i, table_ref: (lax.rem(table_ref[steps + i], 2), 0))
    args = [*amps, *terms, from_down, from_up, *more]
    specs = (
        amp_specs(amps, steps)
        + [fixed(DEPTH, GCOLS)] * 2
        + [block] * 2
        + [fixed(HALF, GCOLS)] * len(more)
    )
    alias = {}
    if result is not None:
        alias = {1 + len(args): 1}
        args.append(result)
        specs.append(pl.BlockSpec(memory_space=pl.ANY))
    return call(
        body,
        2,
        table,
        args,
        specs,
        [f32(HALF, GCOLS), f32(HALF, ABT * TB)],
        [fixed(HALF, GCOLS), pl.BlockSpec(memory_space=pl.ANY)],
        "products_here",
        input_output_aliases=alias,
        scratch_shapes=[pltpu.VMEM((HALF, GCOLS), jnp.float32), pltpu.SemaphoreType.DMA((SIDE,))],
    )


def place(table, theirs, cols, result):
    def body(table_ref, theirs_ref, result_ref, out, sems):
        for copy in write_columns(theirs_ref, out, table_ref, cols, sems):
            copy.wait()

    return call(
        body,
        1,
        table,
        [theirs, result],
        [fixed(HALF, GCOLS), pl.BlockSpec(memory_space=pl.ANY)],
        f32(HALF, ABT * TB),
        pl.BlockSpec(memory_space=pl.ANY),
        "place",
        SMALL_MIB,
        input_output_aliases={2: 0},
        scratch_shapes=[pltpu.SemaphoreType.DMA((SIDE,))],
    )


def per_device(amplitudes, integral_tiles, integral_blocks):
    row, col = lax.axis_index("row"), lax.axis_index("col")
    z, core = row // 2, row % 2
    y, x = col // SIDE, col % SIDE
    a1 = jnp.where(core == 0, x, y)
    a2 = jnp.where(core == 0, y, x)
    wrap = lambda v: lax.rem(v + 2 * SIDE, SIDE)
    block = lambda k, h: 2 * wrap(z + k) + h

    tiles = integral_tiles.reshape(N_ROW, N_COL, TB, TB)
    coords = integral_blocks.reshape(N_ROW, N_COL, 2)[:, :, 0]
    own_rows = jnp.stack([coords[2 * wrap(z - k) + core] for k in range(SIDE)], axis=1)

    dest = lambda s, t: col_of(core, wrap(a1 + s), wrap(a2 + t))
    parts = {
        "rows": [2 * wrap(z - k) + (core + p) % 2 for p in range(2) for k in range(SIDE)],
        "near": [dest(s, 0) for s in range(SIDE)],
        "far1": [dest(s, 1) for s in range(1, SIDE)],
        "far32": [dest(s, t) for t in (3, 2) for s in range(1, SIDE)],
        "away": [block(2, 0), block(2, 1)],
        "next": [block(1, 0), block(1, 1), block(3, 0), block(3, 1)],
        "here": [block(0, 1 - core), block(0, core)],
    }
    for t in range(SIDE):
        parts[f"own{t}"] = [dest(0, t)]
        for c, name in ((core, "mine"), (1 - core, "theirs")):
            b1, b2 = jnp.where(c == 0, x, y), jnp.where(c == 0, y, x)
            parts[f"{name}{t}"] = [
                N_COL * c + col_of(c, wrap(b1 - s), wrap(b2 - t)) for s in range(SIDE)
            ]
    at, length = {}, 0
    for name, values in parts.items():
        at[name], length = length, length + len(values)
    at["places"], at["live"] = length, length + N_COL * SIDE
    table = jnp.concatenate(
        [
            jnp.stack([v for values in parts.values() for v in values]).astype(jnp.int32),
            jnp.where(own_rows >= 0, own_rows % CD_ROW, 0).astype(jnp.int32).reshape(-1),
            (own_rows >= 0).astype(jnp.int32).reshape(-1),
        ]
    )

    first = lambda arrays: [
        lax.ppermute(a, ANYWHERE, plane_shift(True, s)) for s, a in enumerate(arrays, 1)
    ]
    second = lambda array, t: lax.ppermute(array, ANYWHERE, plane_shift(False, t))
    up_z = lambda v: lax.ppermute(v, "row", z_shift(1))
    down_z = lambda v: lax.ppermute(v, "row", z_shift(-1))

    panels = [amplitudes] + [
        lax.ppermute(amplitudes, "row", z_shift(k)) for k in (1, 2, 3)
    ]
    near = pick_tiles(tiles, table, at["near"], at["rows"], 4)
    group0 = [near[0]] + first(near[1:])
    chosen = choose(panels, after(table, group0), at["places"], at["live"])
    own = lax.all_to_all(chosen, "col", split_axis=0, concat_axis=0, tiled=True)
    own = own.reshape(-1, SIDE * TB)
    amps = [own, lax.ppermute(own, "row", OTHER_CORE)]

    join = lambda t, passed, *deps: join_tiles(
        tiles, after(table, *deps), at[f"own{t}"], at["rows"], passed
    )

    def away(weights, *deps):
        half_up, half_down, *terms = products_away(after(table, *deps), at["away"], amps, weights)
        return (terms, up_z(half_up), down_z(half_down)), half_up

    def onward(state, *deps):
        terms = state[0]
        up, down = products_next(after(table, *deps), at["next"], amps, *state)
        return (terms, up_z(up), down_z(down)), up

    def here(state, t, result, before, *deps):
        theirs, result = products_here(
            after(table, *deps), at["here"], amps, *state, at[f"mine{t}"], result, before
        )
        return result, (lax.ppermute(theirs, "row", OTHER_CORE), at[f"theirs{t}"])

    far1 = pick_tiles(tiles, after(table, own), at["far1"], at["rows"], 3)
    passed1 = first(far1)
    g0, sent = away(group0, far1)
    far32 = pick_tiles(tiles, after(table, sent), at["far32"], at["rows"], 6)
    joined1 = join(1, passed1, far32)
    moved1 = second(joined1, 1)
    passed3 = first(after(far32[:3], passed1))
    g0, sent = onward(g0, joined1)
    joined3 = join(3, passed3, sent)
    moved3 = second(joined3, 3)
    passed2 = first(after(far32[3:], passed3))
    g1, sent = away([moved1], joined3)
    result, before = here(g0, 0, None, None, sent)
    g1, sent = onward(g1, result)
    joined2 = join(2, passed2, sent)
    moved2 = second(joined2, 2)
    g3, sent = away([moved3], joined2)
    g2, sent = away([moved2], sent)
    result, before = here(g1, 1, result, before, sent)
    g3, sent = onward(g3, result)
    g2, sent = onward(g2, sent)
    result, before = here(g3, 3, result, before, sent)
    result, before = here(g2, 2, result, before)
    return place(table, *before, result)


def solution(mesh):
    placed = (
        P("col", "row"),
        P(None, ("row", "col"), None, None, None),
        P(None, ("row", "col"), None, None),
    )
    return jax.shard_map(
        per_device, mesh=mesh, in_specs=placed, out_specs=P("row", "col"), check_vma=False
    )
```

```python
import jax
import jax.numpy as jnp
from jax import lax
from jax.experimental import pallas as pl
from jax.experimental.pallas import tpu as pltpu
from jax.sharding import PartitionSpec as P

TB = 128
ABT = 32
CD_ROW = 8
SIDE = 4
N_ROW = 8
N_COL = 16
HALF = 256
PLANE = 512
GCOLS = SIDE * TB
ANYWHERE = ("row", "col")


def col_of(core, a1, a2):
    return jnp.where(core == 0, a2 * SIDE + a1, a1 * SIDE + a2)


def z_shift(step):
    return [(r, ((r // 2 + step) % SIDE) * 2 + r % 2) for r in range(N_ROW)]


def plane_shift(first, step):
    pairs = []
    for r in range(N_ROW):
        for c in range(N_COL):
            y, x = c // SIDE, c % SIDE
            if (r % 2 == 0) == first:
                x = (x + step) % SIDE
            else:
                y = (y + step) % SIDE
            pairs.append((r * N_COL + c, r * N_COL + y * SIDE + x))
    return pairs


def after(values, *deps):
    return lax.optimization_barrier((values, deps))[0]


OTHER_CORE = [(r, r ^ 1) for r in range(N_ROW)]


def params(mib):
    return pltpu.CompilerParams(
        dimension_semantics=("arbitrary",), vmem_limit_bytes=mib * 1024 * 1024
    )


SMALL = pl.CostEstimate(flops=0, bytes_accessed=1024, transcendentals=0)
BIG_MIB, SMALL_MIB = 24, 24


def call(body, grid, table, args, in_specs, out_shape, out_specs, name, mib=BIG_MIB, **more):
    scratch = more.pop("scratch_shapes", [])
    return pl.pallas_call(
        body,
        out_shape=out_shape,
        grid_spec=pltpu.PrefetchScalarGridSpec(
            num_scalar_prefetch=1,
            grid=(grid,),
            in_specs=in_specs,
            out_specs=out_specs,
            scratch_shapes=scratch,
        ),
        compiler_params=params(mib),
        cost_estimate=SMALL,
        name=name,
        **more,
    )(table, *args)


def f32(*shape):
    return jax.ShapeDtypeStruct(shape, jnp.float32)


def fixed(*shape):
    return pl.BlockSpec(shape, lambda j, table: (0,) * len(shape))


def pick_tiles(tiles, table, cols, rows, count):
    def body(table_ref, tiles_ref, *outs):
        for i in range(count):

            @pl.when(pl.program_id(0) == i)
            def _(out=outs[i]):
                for n in range(N_ROW):
                    out[0, n] = tiles_ref[table_ref[rows + n], 0]

    return call(
        body,
        count,
        table,
        [tiles],
        [pl.BlockSpec((N_ROW, 1, TB, TB), lambda j, table_ref: (0, table_ref[cols + j], 0, 0))],
        [f32(1, N_ROW, TB, TB)] * count,
        [fixed(1, N_ROW, TB, TB)] * count,
        "pick_tiles",
    )


def join_tiles(tiles, table, col, rows, passed):
    def body(table_ref, tiles_ref, *refs):
        ins, out = refs[:-1], refs[-1]

        @pl.when(pl.program_id(0) == 0)
        def _():
            for n in range(N_ROW):
                out[0, n] = tiles_ref[table_ref[rows + n], 0]

        for s in range(1, SIDE):

            @pl.when(pl.program_id(0) == s)
            def _(s=s):
                out[...] = ins[s - 1][...]

    block = (1, N_ROW, TB, TB)
    return call(
        body,
        SIDE,
        table,
        [tiles, *passed],
        [pl.BlockSpec((N_ROW, 1, TB, TB), lambda j, table_ref: (0, table_ref[col], 0, 0))]
        + [fixed(*block)] * len(passed),
        f32(SIDE, N_ROW, TB, TB),
        pl.BlockSpec(block, lambda j, table_ref: (j, 0, 0, 0)),
        "join_tiles",
    )


def choose(panels, table, places, live):
    n_ij = panels[0].shape[0]

    def body(table_ref, *refs):
        c = pl.program_id(0)
        out = refs[SIDE]
        for k in range(SIDE):
            at = pl.multiple_of(table_ref[places + c * SIDE + k] * TB, TB)
            tile = refs[k][:, pl.ds(at, TB)]
            listed = table_ref[live + c * SIDE + k] > 0
            out[0, :, k * TB : (k + 1) * TB] = jnp.where(listed, tile, 0.0)

    return call(
        body,
        N_COL,
        table,
        panels,
        [fixed(*p.shape) for p in panels],
        f32(N_COL, n_ij, SIDE * TB),
        pl.BlockSpec((1, n_ij, SIDE * TB), lambda c, table_ref: (c, 0, 0)),
        "choose",
        SMALL_MIB,
    )


def split(x):
    high = x.astype(jnp.bfloat16)
    return high, (x - high.astype(jnp.float32)).astype(jnp.bfloat16)


def product(a_refs, high_ref, low_ref):
    high, low = split(jnp.concatenate([ref[...] for ref in a_refs], axis=1))
    total = jnp.dot(high, low_ref[...], preferred_element_type=jnp.float32)
    total += jnp.dot(low, high_ref[...], preferred_element_type=jnp.float32)
    return total + jnp.dot(high, high_ref[...], preferred_element_type=jnp.float32)


def amp_specs(amps, steps):
    return [
        pl.BlockSpec((HALF, a.shape[1]), lambda i, table_ref: (table_ref[steps + i], 0))
        for a in amps
    ]


DEPTH = N_ROW * TB
TERM = jax.ShapeDtypeStruct((DEPTH, GCOLS), jnp.bfloat16)


def products_away(table, steps, amps, weights):
    def body(table_ref, *refs):
        a_refs, w_refs = refs[: len(amps)], refs[len(amps) : -4]
        half_up, half_down, high_ref, low_ref = refs[-4:]
        i = pl.program_id(0)

        @pl.when(i == 0)
        def _():
            s = 0
            for ref in w_refs:
                for m in range(ref.shape[0]):
                    high, low = split(ref[m].reshape(DEPTH, TB))
                    high_ref[:, s * TB : (s + 1) * TB] = high
                    low_ref[:, s * TB : (s + 1) * TB] = low
                    s += 1

        total = product(a_refs, high_ref, low_ref)

        @pl.when(i == 0)
        def _():
            half_up[...] = total

        @pl.when(i == 1)
        def _():
            half_down[...] = total

    return call(
        body,
        2,
        table,
        [*amps, *weights],
        amp_specs(amps, steps) + [fixed(*w.shape) for w in weights],
        [f32(HALF, GCOLS)] * 2 + [TERM] * 2,
        [fixed(HALF, GCOLS)] * 2 + [fixed(DEPTH, GCOLS)] * 2,
        "products_away",
    )


def products_next(table, steps, amps, terms, from_down, from_up):
    def body(table_ref, *refs):
        a_refs = refs[: len(amps)]
        high_ref, low_ref, f_ref, g_ref, up, down = refs[len(amps) :]
        i = pl.program_id(0)
        total = product(a_refs, high_ref, low_ref)

        @pl.when(i == 0)
        def _():
            up[...] = total + f_ref[...]

        @pl.when(i == 1)
        def _():
            up[...] = total

        @pl.when(i == 2)
        def _():
            down[...] = total

        @pl.when(i == 3)
        def _():
            down[...] = total + g_ref[...]

    return call(
        body,
        4,
        table,
        [*amps, *terms, from_down, from_up],
        amp_specs(amps, steps) + [fixed(DEPTH, GCOLS)] * 2 + [fixed(HALF, GCOLS)] * 2,
        [f32(PLANE, GCOLS)] * 2,
        [
            pl.BlockSpec((HALF, GCOLS), lambda i, table_ref: (jnp.minimum(i, 1), 0)),
            pl.BlockSpec((HALF, GCOLS), lambda i, table_ref: (jnp.maximum(i - 2, 0), 0)),
        ],
        "products_next",
    )


def write_columns(source, out, table_ref, cols, sems):
    copies = []
    for s in range(SIDE):
        at = pl.multiple_of(table_ref[cols + s] * TB, TB)
        copies.append(
            pltpu.make_async_copy(
                source.at[:, pl.ds(s * TB, TB)], out.at[:, pl.ds(at, TB)], sems.at[s]
            )
        )
        copies[-1].start()
    return copies


def products_here(table, steps, amps, terms, from_down, from_up, cols, result, before):
    more = [] if before is None else [before[0]]

    def body(table_ref, *refs):
        a_refs = refs[: len(amps)]
        high_ref, low_ref, f_ref, g_ref = refs[len(amps) : len(amps) + 4]
        theirs, out, mine, sems = refs[-4:]
        i = pl.program_id(0)
        if before is not None:

            @pl.when(i == 0)
            def _():
                copies = write_columns(refs[len(amps) + 4], out, table_ref, before[1], sems)
                for copy in copies:
                    copy.wait()

        total = product(a_refs, high_ref, low_ref) + (f_ref[...] + g_ref[...])

        @pl.when(i == 0)
        def _():
            theirs[...] = total

        @pl.when(i == 1)
        def _():
            mine[...] = total
            for copy in write_columns(mine, out, table_ref, cols, sems):
                copy.wait()

    block = pl.BlockSpec((HALF, GCOLS), lambda i, table_ref: (lax.rem(table_ref[steps + i], 2), 0))
    args = [*amps, *terms, from_down, from_up, *more]
    specs = (
        amp_specs(amps, steps)
        + [fixed(DEPTH, GCOLS)] * 2
        + [block] * 2
        + [fixed(HALF, GCOLS)] * len(more)
    )
    alias = {}
    if result is not None:
        alias = {1 + len(args): 1}
        args.append(result)
        specs.append(pl.BlockSpec(memory_space=pl.ANY))
    return call(
        body,
        2,
        table,
        args,
        specs,
        [f32(HALF, GCOLS), f32(HALF, ABT * TB)],
        [fixed(HALF, GCOLS), pl.BlockSpec(memory_space=pl.ANY)],
        "products_here",
        input_output_aliases=alias,
        scratch_shapes=[pltpu.VMEM((HALF, GCOLS), jnp.float32), pltpu.SemaphoreType.DMA((SIDE,))],
    )


def place(table, theirs, cols, result):
    def body(table_ref, theirs_ref, result_ref, out, sems):
        for copy in write_columns(theirs_ref, out, table_ref, cols, sems):
            copy.wait()

    return call(
        body,
        1,
        table,
        [theirs, result],
        [fixed(HALF, GCOLS), pl.BlockSpec(memory_space=pl.ANY)],
        f32(HALF, ABT * TB),
        pl.BlockSpec(memory_space=pl.ANY),
        "place",
        SMALL_MIB,
        input_output_aliases={2: 0},
        scratch_shapes=[pltpu.SemaphoreType.DMA((SIDE,))],
    )


def per_device(amplitudes, integral_tiles, integral_blocks):
    row, col = lax.axis_index("row"), lax.axis_index("col")
    z, core = row // 2, row % 2
    y, x = col // SIDE, col % SIDE
    a1 = jnp.where(core == 0, x, y)
    a2 = jnp.where(core == 0, y, x)
    wrap = lambda v: lax.rem(v + 2 * SIDE, SIDE)
    block = lambda k, h: 2 * wrap(z + k) + h

    tiles = integral_tiles.reshape(N_ROW, N_COL, TB, TB)
    coords = integral_blocks.reshape(N_ROW, N_COL, 2)[:, :, 0]
    own_rows = jnp.stack([coords[2 * wrap(z - k) + core] for k in range(SIDE)], axis=1)

    dest = lambda s, t: col_of(core, wrap(a1 + s), wrap(a2 + t))
    parts = {
        "rows": [2 * wrap(z - k) + (core + p) % 2 for p in range(2) for k in range(SIDE)],
        "near": [dest(s, 0) for s in range(SIDE)],
        "far1": [dest(s, 1) for s in range(1, SIDE)],
        "far32": [dest(s, t) for t in (3, 2) for s in range(1, SIDE)],
        "away": [block(2, 0), block(2, 1)],
        "next": [block(1, 0), block(1, 1), block(3, 0), block(3, 1)],
        "here": [block(0, 1 - core), block(0, core)],
    }
    for t in range(SIDE):
        parts[f"own{t}"] = [dest(0, t)]
        for c, name in ((core, "mine"), (1 - core, "theirs")):
            b1, b2 = jnp.where(c == 0, x, y), jnp.where(c == 0, y, x)
            parts[f"{name}{t}"] = [
                N_COL * c + col_of(c, wrap(b1 - s), wrap(b2 - t)) for s in range(SIDE)
            ]
    at, length = {}, 0
    for name, values in parts.items():
        at[name], length = length, length + len(values)
    at["places"], at["live"] = length, length + N_COL * SIDE
    table = jnp.concatenate(
        [
            jnp.stack([v for values in parts.values() for v in values]).astype(jnp.int32),
            jnp.where(own_rows >= 0, own_rows % CD_ROW, 0).astype(jnp.int32).reshape(-1),
            (own_rows >= 0).astype(jnp.int32).reshape(-1),
        ]
    )

    first = lambda arrays: [
        lax.ppermute(a, ANYWHERE, plane_shift(True, s)) for s, a in enumerate(arrays, 1)
    ]
    second = lambda array, t: lax.ppermute(array, ANYWHERE, plane_shift(False, t))
    up_z = lambda v: lax.ppermute(v, "row", z_shift(1))
    down_z = lambda v: lax.ppermute(v, "row", z_shift(-1))

    panels = [amplitudes] + [
        lax.ppermute(amplitudes, "row", z_shift(k)) for k in (1, 2, 3)
    ]
    near = pick_tiles(tiles, table, at["near"], at["rows"], 4)
    group0 = [near[0]] + first(near[1:])
    chosen = choose(panels, after(table, group0), at["places"], at["live"])
    own = lax.all_to_all(chosen, "col", split_axis=0, concat_axis=0, tiled=True)
    own = own.reshape(-1, SIDE * TB)
    amps = [own, lax.ppermute(own, "row", OTHER_CORE)]

    join = lambda t, passed, *deps: join_tiles(
        tiles, after(table, *deps), at[f"own{t}"], at["rows"], passed
    )

    def away(weights, *deps):
        half_up, half_down, *terms = products_away(after(table, *deps), at["away"], amps, weights)
        return (terms, up_z(half_up), down_z(half_down)), half_up

    def onward(state, *deps):
        terms = state[0]
        up, down = products_next(after(table, *deps), at["next"], amps, *state)
        return (terms, up_z(up), down_z(down)), up

    def here(state, t, result, before, *deps):
        theirs, result = products_here(
            after(table, *deps), at["here"], amps, *state, at[f"mine{t}"], result, before
        )
        return result, (lax.ppermute(theirs, "row", OTHER_CORE), at[f"theirs{t}"])

    far1 = pick_tiles(tiles, after(table, own), at["far1"], at["rows"], 3)
    passed1 = first(far1)
    g0, sent = away(group0, far1)
    far32 = pick_tiles(tiles, after(table, sent), at["far32"], at["rows"], 6)
    joined1 = join(1, passed1, far32)
    moved1 = second(joined1, 1)
    passed3 = first(after(far32[:3], passed1))
    g0, sent = onward(g0, joined1)
    joined3 = join(3, passed3, sent)
    moved3 = second(joined3, 3)
    passed2 = first(after(far32[3:], passed3))
    g1, sent = away([moved1], joined3)
    result, before = here(g0, 0, None, None, sent)
    g1, sent = onward(g1, result)
    joined2 = join(2, passed2, sent)
    moved2 = second(joined2, 2)
    g3, sent = away([moved3], joined2)
    g2, sent = away([moved2], sent)
    result, before = here(g1, 1, result, before, sent)
    g3, sent = onward(g3, result)
    g2, sent = onward(g2, sent)
    result, before = here(g3, 3, result, before, sent)
    result, before = here(g2, 2, result, before)
    return place(table, *before, result)


def solution(mesh):
    placed = (
        P("col", "row"),
        P(None, ("row", "col"), None, None, None),
        P(None, ("row", "col"), None, None),
    )
    return jax.shard_map(
        per_device, mesh=mesh, in_specs=placed, out_specs=P("row", "col"), check_vma=False
    )
```

```python
import jax
import jax.numpy as jnp
from jax import lax
from jax.experimental import pallas as pl
from jax.experimental.pallas import tpu as pltpu
from jax.sharding import PartitionSpec as P

TB = 128
ABT = 32
CD_ROW = 8
SIDE = 4
N_ROW = 8
N_COL = 16
HALF = 256
PLANE = 512
GCOLS = SIDE * TB
ANYWHERE = ("row", "col")


def col_of(core, a1, a2):
    return jnp.where(core == 0, a2 * SIDE + a1, a1 * SIDE + a2)


def z_shift(step):
    return [(r, ((r // 2 + step) % SIDE) * 2 + r % 2) for r in range(N_ROW)]


def plane_shift(first, step):
    pairs = []
    for r in range(N_ROW):
        for c in range(N_COL):
            y, x = c // SIDE, c % SIDE
            if (r % 2 == 0) == first:
                x = (x + step) % SIDE
            else:
                y = (y + step) % SIDE
            pairs.append((r * N_COL + c, r * N_COL + y * SIDE + x))
    return pairs


def after(values, *deps):
    return lax.optimization_barrier((values, deps))[0]


OTHER_CORE = [(r, r ^ 1) for r in range(N_ROW)]


def params(mib):
    return pltpu.CompilerParams(
        dimension_semantics=("arbitrary",), vmem_limit_bytes=mib * 1024 * 1024
    )


SMALL = pl.CostEstimate(flops=0, bytes_accessed=1024, transcendentals=0)
BIG_MIB, SMALL_MIB = 20, 20


def call(body, grid, table, args, in_specs, out_shape, out_specs, name, mib=BIG_MIB, **more):
    scratch = more.pop("scratch_shapes", [])
    return pl.pallas_call(
        body,
        out_shape=out_shape,
        grid_spec=pltpu.PrefetchScalarGridSpec(
            num_scalar_prefetch=1,
            grid=(grid,),
            in_specs=in_specs,
            out_specs=out_specs,
            scratch_shapes=scratch,
        ),
        compiler_params=params(mib),
        cost_estimate=SMALL,
        name=name,
        **more,
    )(table, *args)


def f32(*shape):
    return jax.ShapeDtypeStruct(shape, jnp.float32)


def fixed(*shape):
    return pl.BlockSpec(shape, lambda j, table: (0,) * len(shape))


def pick_tiles(tiles, table, cols, rows, count):
    def body(table_ref, tiles_ref, *outs):
        for i in range(count):

            @pl.when(pl.program_id(0) == i)
            def _(out=outs[i]):
                for n in range(N_ROW):
                    out[0, n] = tiles_ref[table_ref[rows + n], 0]

    return call(
        body,
        count,
        table,
        [tiles],
        [pl.BlockSpec((N_ROW, 1, TB, TB), lambda j, table_ref: (0, table_ref[cols + j], 0, 0))],
        [f32(1, N_ROW, TB, TB)] * count,
        [fixed(1, N_ROW, TB, TB)] * count,
        "pick_tiles",
    )


def join_tiles(tiles, table, col, rows, passed):
    def body(table_ref, tiles_ref, *refs):
        ins, out = refs[:-1], refs[-1]

        @pl.when(pl.program_id(0) == 0)
        def _():
            for n in range(N_ROW):
                out[0, n] = tiles_ref[table_ref[rows + n], 0]

        for s in range(1, SIDE):

            @pl.when(pl.program_id(0) == s)
            def _(s=s):
                out[...] = ins[s - 1][...]

    block = (1, N_ROW, TB, TB)
    return call(
        body,
        SIDE,
        table,
        [tiles, *passed],
        [pl.BlockSpec((N_ROW, 1, TB, TB), lambda j, table_ref: (0, table_ref[col], 0, 0))]
        + [fixed(*block)] * len(passed),
        f32(SIDE, N_ROW, TB, TB),
        pl.BlockSpec(block, lambda j, table_ref: (j, 0, 0, 0)),
        "join_tiles",
    )


def choose(panels, table, places, live):
    n_ij = panels[0].shape[0]

    def body(table_ref, *refs):
        c = pl.program_id(0)
        out = refs[SIDE]
        for k in range(SIDE):
            at = pl.multiple_of(table_ref[places + c * SIDE + k] * TB, TB)
            tile = refs[k][:, pl.ds(at, TB)]
            listed = table_ref[live + c * SIDE + k] > 0
            out[0, :, k * TB : (k + 1) * TB] = jnp.where(listed, tile, 0.0)

    return call(
        body,
        N_COL,
        table,
        panels,
        [fixed(*p.shape) for p in panels],
        f32(N_COL, n_ij, SIDE * TB),
        pl.BlockSpec((1, n_ij, SIDE * TB), lambda c, table_ref: (c, 0, 0)),
        "choose",
        SMALL_MIB,
    )


def split(x):
    high = x.astype(jnp.bfloat16)
    return high, (x - high.astype(jnp.float32)).astype(jnp.bfloat16)


def product(a_refs, high_ref, low_ref):
    high, low = split(jnp.concatenate([ref[...] for ref in a_refs], axis=1))
    total = jnp.dot(high, low_ref[...], preferred_element_type=jnp.float32)
    total += jnp.dot(low, high_ref[...], preferred_element_type=jnp.float32)
    return total + jnp.dot(high, high_ref[...], preferred_element_type=jnp.float32)


def amp_specs(amps, steps):
    return [
        pl.BlockSpec((HALF, a.shape[1]), lambda i, table_ref: (table_ref[steps + i], 0))
        for a in amps
    ]


DEPTH = N_ROW * TB
TERM = jax.ShapeDtypeStruct((DEPTH, GCOLS), jnp.bfloat16)


def products_away(table, steps, amps, weights):
    def body(table_ref, *refs):
        a_refs, w_refs = refs[: len(amps)], refs[len(amps) : -4]
        half_up, half_down, high_ref, low_ref = refs[-4:]
        i = pl.program_id(0)

        @pl.when(i == 0)
        def _():
            s = 0
            for ref in w_refs:
                for m in range(ref.shape[0]):
                    high, low = split(ref[m].reshape(DEPTH, TB))
                    high_ref[:, s * TB : (s + 1) * TB] = high
                    low_ref[:, s * TB : (s + 1) * TB] = low
                    s += 1

        total = product(a_refs, high_ref, low_ref)

        @pl.when(i == 0)
        def _():
            half_up[...] = total

        @pl.when(i == 1)
        def _():
            half_down[...] = total

    return call(
        body,
        2,
        table,
        [*amps, *weights],
        amp_specs(amps, steps) + [fixed(*w.shape) for w in weights],
        [f32(HALF, GCOLS)] * 2 + [TERM] * 2,
        [fixed(HALF, GCOLS)] * 2 + [fixed(DEPTH, GCOLS)] * 2,
        "products_away",
    )


def products_next(table, steps, amps, terms, from_down, from_up):
    def body(table_ref, *refs):
        a_refs = refs[: len(amps)]
        high_ref, low_ref, f_ref, g_ref, up, down = refs[len(amps) :]
        i = pl.program_id(0)
        total = product(a_refs, high_ref, low_ref)

        @pl.when(i == 0)
        def _():
            up[...] = total + f_ref[...]

        @pl.when(i == 1)
        def _():
            up[...] = total

        @pl.when(i == 2)
        def _():
            down[...] = total

        @pl.when(i == 3)
        def _():
            down[...] = total + g_ref[...]

    return call(
        body,
        4,
        table,
        [*amps, *terms, from_down, from_up],
        amp_specs(amps, steps) + [fixed(DEPTH, GCOLS)] * 2 + [fixed(HALF, GCOLS)] * 2,
        [f32(PLANE, GCOLS)] * 2,
        [
            pl.BlockSpec((HALF, GCOLS), lambda i, table_ref: (jnp.minimum(i, 1), 0)),
            pl.BlockSpec((HALF, GCOLS), lambda i, table_ref: (jnp.maximum(i - 2, 0), 0)),
        ],
        "products_next",
    )


def write_columns(source, out, table_ref, cols, sems):
    copies = []
    for s in range(SIDE):
        at = pl.multiple_of(table_ref[cols + s] * TB, TB)
        copies.append(
            pltpu.make_async_copy(
                source.at[:, pl.ds(s * TB, TB)], out.at[:, pl.ds(at, TB)], sems.at[s]
            )
        )
        copies[-1].start()
    return copies


def products_here(table, steps, amps, terms, from_down, from_up, cols, result, before):
    more = [] if before is None else [before[0]]

    def body(table_ref, *refs):
        a_refs = refs[: len(amps)]
        high_ref, low_ref, f_ref, g_ref = refs[len(amps) : len(amps) + 4]
        theirs, out, mine, sems = refs[-4:]
        i = pl.program_id(0)
        if before is not None:

            @pl.when(i == 0)
            def _():
                copies = write_columns(refs[len(amps) + 4], out, table_ref, before[1], sems)
                for copy in copies:
                    copy.wait()

        total = product(a_refs, high_ref, low_ref) + (f_ref[...] + g_ref[...])

        @pl.when(i == 0)
        def _():
            theirs[...] = total

        @pl.when(i == 1)
        def _():
            mine[...] = total
            for copy in write_columns(mine, out, table_ref, cols, sems):
                copy.wait()

    block = pl.BlockSpec((HALF, GCOLS), lambda i, table_ref: (lax.rem(table_ref[steps + i], 2), 0))
    args = [*amps, *terms, from_down, from_up, *more]
    specs = (
        amp_specs(amps, steps)
        + [fixed(DEPTH, GCOLS)] * 2
        + [block] * 2
        + [fixed(HALF, GCOLS)] * len(more)
    )
    alias = {}
    if result is not None:
        alias = {1 + len(args): 1}
        args.append(result)
        specs.append(pl.BlockSpec(memory_space=pl.ANY))
    return call(
        body,
        2,
        table,
        args,
        specs,
        [f32(HALF, GCOLS), f32(HALF, ABT * TB)],
        [fixed(HALF, GCOLS), pl.BlockSpec(memory_space=pl.ANY)],
        "products_here",
        input_output_aliases=alias,
        scratch_shapes=[pltpu.VMEM((HALF, GCOLS), jnp.float32), pltpu.SemaphoreType.DMA((SIDE,))],
    )


def place(table, theirs, cols, result):
    def body(table_ref, theirs_ref, result_ref, out, sems):
        for copy in write_columns(theirs_ref, out, table_ref, cols, sems):
            copy.wait()

    return call(
        body,
        1,
        table,
        [theirs, result],
        [fixed(HALF, GCOLS), pl.BlockSpec(memory_space=pl.ANY)],
        f32(HALF, ABT * TB),
        pl.BlockSpec(memory_space=pl.ANY),
        "place",
        SMALL_MIB,
        input_output_aliases={2: 0},
        scratch_shapes=[pltpu.SemaphoreType.DMA((SIDE,))],
    )


def per_device(amplitudes, integral_tiles, integral_blocks):
    row, col = lax.axis_index("row"), lax.axis_index("col")
    z, core = row // 2, row % 2
    y, x = col // SIDE, col % SIDE
    a1 = jnp.where(core == 0, x, y)
    a2 = jnp.where(core == 0, y, x)
    wrap = lambda v: lax.rem(v + 2 * SIDE, SIDE)
    block = lambda k, h: 2 * wrap(z + k) + h

    tiles = integral_tiles.reshape(N_ROW, N_COL, TB, TB)
    coords = integral_blocks.reshape(N_ROW, N_COL, 2)[:, :, 0]
    own_rows = jnp.stack([coords[2 * wrap(z - k) + core] for k in range(SIDE)], axis=1)

    dest = lambda s, t: col_of(core, wrap(a1 + s), wrap(a2 + t))
    parts = {
        "rows": [2 * wrap(z - k) + (core + p) % 2 for p in range(2) for k in range(SIDE)],
        "near": [dest(s, 0) for s in range(SIDE)],
        "far1": [dest(s, 1) for s in range(1, SIDE)],
        "far32": [dest(s, t) for t in (3, 2) for s in range(1, SIDE)],
        "away": [block(2, 0), block(2, 1)],
        "next": [block(1, 0), block(1, 1), block(3, 0), block(3, 1)],
        "here": [block(0, 1 - core), block(0, core)],
    }
    for t in range(SIDE):
        parts[f"own{t}"] = [dest(0, t)]
        for c, name in ((core, "mine"), (1 - core, "theirs")):
            b1, b2 = jnp.where(c == 0, x, y), jnp.where(c == 0, y, x)
            parts[f"{name}{t}"] = [
                N_COL * c + col_of(c, wrap(b1 - s), wrap(b2 - t)) for s in range(SIDE)
            ]
    at, length = {}, 0
    for name, values in parts.items():
        at[name], length = length, length + len(values)
    at["places"], at["live"] = length, length + N_COL * SIDE
    table = jnp.concatenate(
        [
            jnp.stack([v for values in parts.values() for v in values]).astype(jnp.int32),
            jnp.where(own_rows >= 0, own_rows % CD_ROW, 0).astype(jnp.int32).reshape(-1),
            (own_rows >= 0).astype(jnp.int32).reshape(-1),
        ]
    )

    first = lambda arrays: [
        lax.ppermute(a, ANYWHERE, plane_shift(True, s)) for s, a in enumerate(arrays, 1)
    ]
    second = lambda array, t: lax.ppermute(array, ANYWHERE, plane_shift(False, t))
    up_z = lambda v: lax.ppermute(v, "row", z_shift(1))
    down_z = lambda v: lax.ppermute(v, "row", z_shift(-1))

    panels = [amplitudes] + [
        lax.ppermute(amplitudes, "row", z_shift(k)) for k in (1, 2, 3)
    ]
    near = pick_tiles(tiles, table, at["near"], at["rows"], 4)
    group0 = [near[0]] + first(near[1:])
    chosen = choose(panels, after(table, group0), at["places"], at["live"])
    own = lax.all_to_all(chosen, "col", split_axis=0, concat_axis=0, tiled=True)
    own = own.reshape(-1, SIDE * TB)
    amps = [own, lax.ppermute(own, "row", OTHER_CORE)]

    join = lambda t, passed, *deps: join_tiles(
        tiles, after(table, *deps), at[f"own{t}"], at["rows"], passed
    )

    def away(weights, *deps):
        half_up, half_down, *terms = products_away(after(table, *deps), at["away"], amps, weights)
        return (terms, up_z(half_up), down_z(half_down)), half_up

    def onward(state, *deps):
        terms = state[0]
        up, down = products_next(after(table, *deps), at["next"], amps, *state)
        return (terms, up_z(up), down_z(down)), up

    def here(state, t, result, before, *deps):
        theirs, result = products_here(
            after(table, *deps), at["here"], amps, *state, at[f"mine{t}"], result, before
        )
        return result, (lax.ppermute(theirs, "row", OTHER_CORE), at[f"theirs{t}"])

    far1 = pick_tiles(tiles, after(table, own), at["far1"], at["rows"], 3)
    passed1 = first(far1)
    g0, sent = away(group0, far1)
    far32 = pick_tiles(tiles, after(table, sent), at["far32"], at["rows"], 6)
    joined1 = join(1, passed1, far32)
    moved1 = second(joined1, 1)
    passed3 = first(after(far32[:3], passed1))
    g0, sent = onward(g0, joined1)
    joined3 = join(3, passed3, sent)
    moved3 = second(joined3, 3)
    passed2 = first(after(far32[3:], passed3))
    g1, sent = away([moved1], joined3)
    result, before = here(g0, 0, None, None, sent)
    g1, sent = onward(g1, result)
    joined2 = join(2, passed2, sent)
    moved2 = second(joined2, 2)
    g3, sent = away([moved3], joined2)
    g2, sent = away([moved2], sent)
    result, before = here(g1, 1, result, before, sent)
    g3, sent = onward(g3, result)
    g2, sent = onward(g2, sent)
    result, before = here(g3, 3, result, before, sent)
    result, before = here(g2, 2, result, before)
    return place(table, *before, result)


def solution(mesh):
    placed = (
        P("col", "row"),
        P(None, ("row", "col"), None, None, None),
        P(None, ("row", "col"), None, None),
    )
    return jax.shard_map(
        per_device, mesh=mesh, in_specs=placed, out_specs=P("row", "col"), check_vma=False
    )
```
